512 devices in a mesh: row: 16 (over z, core), col: 32 (over x, y).
Axes of the slice: x: 4, y: 8, z: 8, core: 2. Of those that a mesh axis runs over, the one named last changes fastest.
Arguments:
- hamiltonian: float32 [12288, 12288], P('row', 'col'), may hold values from -5 to 5, as said below
- factor_rows: float32 [128, 12288], P(None, 'col'), may hold values from -0.5 to 3, as said below
Outputs:
- state: float32 [12288, 12288], P('row', 'col')
The draws below stay inside these ranges and needn't reach their ends.
Inputs may be any that keep to these rules, and one draw needn't show every extreme that they name: In global order hamiltonian is symmetric. In global column order, row k of factor_rows is zero at columns before k and lies in 1.5 to 3 at column k.
All inputs are finite; a program needn't handle non-finite values.
Results may differ from the reference program's by a relative error of at most 0.0001.
Values sent between devices are 32-bit elements; how exact they have to be, the bound alone decides.
No kernel may reach another device: no remote copies, remote signals or barrier semaphores. Data moves between devices by JAX's collectives and lax.ppermute only.
A program may use at most 64 MiB of HBM per device.

```python
import jax
import jax.numpy as jnp
from jax import lax

BLOCK = 64
COL_BLOCKS = 6
GRID_ROWS = 16
GRID_COLS = 32
ROW_BLOCKS = 12
ORDER = 12288


def draw_hamiltonian(key, part):
    key = jax.random.fold_in(key, 11)
    sample = jnp.clip(jax.random.normal(key, (ORDER, ORDER), jnp.float32), -5.0, 5.0)
    symmetric = (sample + sample.T) * 0.5
    return symmetric.reshape(ROW_BLOCKS, GRID_ROWS, BLOCK, COL_BLOCKS, GRID_COLS, BLOCK).transpose(1, 0, 2, 4, 3, 5).reshape(ORDER, ORDER)


def draw_factor_rows(key, part):
    key = jax.random.fold_in(key, 23)
    off_key, diag_key = jax.random.split(key)
    shape = (2 * BLOCK, ORDER)
    spread = jnp.clip(0.1 * jax.random.normal(off_key, shape, jnp.float32), -0.5, 0.5)
    diagonal = jax.random.uniform(diag_key, shape, jnp.float32, 1.5, 3.0)
    row_pos = jnp.arange(2 * BLOCK, dtype=jnp.int32)[:, None]
    col_pos = jnp.arange(ORDER, dtype=jnp.int32)[None, :]
    entries = jnp.where(col_pos == row_pos, diagonal, jnp.where(col_pos > row_pos, spread, 0.0))
    return entries.reshape(2 * BLOCK, COL_BLOCKS, GRID_COLS, BLOCK).transpose(0, 2, 1, 3).reshape(2 * BLOCK, ORDER)


def setup_inputs(seed: int = 0) -> dict:
    arg_keys = jax.random.split(jax.random.key(seed), 3)
    return {
        "hamiltonian": draw_hamiltonian(jax.random.fold_in(arg_keys[2], 71), 0),
        "factor_rows": draw_factor_rows(jax.random.fold_in(arg_keys[2], 71), 0),
    }


def matmul(left_side, right_side):
    return jnp.dot(left_side, right_side, precision=lax.Precision.HIGHEST, preferred_element_type=jnp.float32)


def inner(left_side, right_side):
    return lax.dot_general(left_side, right_side, (((0,), (0,)), ((), ())), precision=lax.Precision.HIGHEST, preferred_element_type=jnp.float32)


def upper_inverse(factor):
    width = factor.shape[0]
    diag_entries = jnp.diagonal(factor)
    power = -(jnp.triu(factor, 1) / diag_entries[:, None])
    total = jnp.eye(width, dtype=factor.dtype) + power
    for _ in range((width - 1).bit_length() - 1):
        power = matmul(power, power)
        total = total + matmul(total, power)
    return total / diag_entries[None, :]


def left_solve(factor, right_side):
    return inner(upper_inverse(factor), right_side)


def right_solve(factor, left_side):
    return matmul(left_side, upper_inverse(factor))


def congruence(factor, matrix):
    inverse = upper_inverse(factor)
    return matmul(inner(inverse, matrix), inverse)


def panel_rest(diag_factor, result, panel_rows, factor_cols):
    solved = left_solve(diag_factor, panel_rows)
    shifted = matmul(result, factor_cols)
    halfway = solved - 0.5 * shifted
    pending = halfway - 0.5 * shifted
    return halfway, pending


def reference(hamiltonian, factor_rows):
    block_width = BLOCK
    double_width = 2 * BLOCK
    matrix = hamiltonian.reshape(GRID_ROWS, ROW_BLOCKS, block_width, GRID_COLS, COL_BLOCKS, block_width).transpose(1, 0, 2, 4, 3, 5).reshape(ORDER, ORDER)
    upper = factor_rows.reshape(double_width, GRID_COLS, COL_BLOCKS, block_width).transpose(0, 2, 1, 3).reshape(double_width, ORDER)
    lead_upper = upper[:block_width]
    next_upper = upper[block_width:]
    lead_factor = lead_upper[:, :block_width]
    lead_result = congruence(lead_factor, matrix[:block_width, :block_width])
    lead_half, lead_pending = panel_rest(lead_factor, lead_result, matrix[:block_width, block_width:], lead_upper[:, block_width:])
    product = matmul(lead_upper[:, block_width:].T, lead_half)
    updated = matrix[block_width:, block_width:] - (product + product.T)
    next_diag = next_upper[:, block_width:double_width]
    couple_result = right_solve(next_diag, lead_pending[:, :block_width])
    lead_remain = lead_pending[:, block_width:] - matmul(couple_result, next_upper[:, double_width:])
    next_result = congruence(next_diag, updated[:block_width, :block_width])
    next_half, next_pending = panel_rest(next_diag, next_result, updated[:block_width, block_width:], next_upper[:, double_width:])
    product = matmul(next_upper[:, double_width:].T, next_half)
    trailing = updated[block_width:, block_width:] - (product + product.T)
    lead_top = jnp.concatenate([lead_result, couple_result, lead_remain], 1)
    next_top = jnp.concatenate([matrix[block_width:double_width, :block_width], next_result, next_pending], 1)
    bottom = jnp.concatenate([matrix[double_width:, :double_width], trailing], 1)
    whole = jnp.concatenate([lead_top, next_top, bottom], 0)
    return whole.reshape(ROW_BLOCKS, GRID_ROWS, block_width, COL_BLOCKS, GRID_COLS, block_width).transpose(1, 0, 2, 4, 3, 5).reshape(ORDER, ORDER)
```

```python
import jax
import jax.numpy as jnp
from jax import lax
from jax.experimental import pallas as pl
from jax.experimental.pallas import tpu as pltpu
from jax.sharding import PartitionSpec as P

BLOCK = 64
WIDE = 2 * BLOCK
EXACT = lax.Precision.HIGHEST


def dot(left, right):
    return jnp.dot(left, right, precision=EXACT, preferred_element_type=jnp.float32)


def inner(left, right):
    return lax.dot_general(
        left, right, (((0,), (0,)), ((), ())), precision=EXACT, preferred_element_type=jnp.float32
    )


def wide_inverse(factor):
    row = lax.broadcasted_iota(jnp.int32, (WIDE, WIDE), 0)
    col = lax.broadcasted_iota(jnp.int32, (WIDE, WIDE), 1)
    on_diag = jnp.where(row == col, factor, 0.0)
    diag_col = jnp.sum(on_diag, axis=1, keepdims=True)
    diag_row = jnp.sum(on_diag, axis=0, keepdims=True)
    same = (row < BLOCK) == (col < BLOCK)
    power = jnp.where((row < col) & same, -factor / diag_col, 0.0)
    total = jnp.where(row == col, 1.0, power)
    for _ in range(5):
        power = dot(power, power)
        total = total + dot(total, power)
    total = total / diag_row
    couple = jnp.where((row < BLOCK) & (col >= BLOCK), factor, 0.0)
    return total - dot(total, dot(couple, total))


def body(
    place, h_ref, rj_ref, hj_ref, ra_ref, rb_ref, ha_ref, hb_ref, factor_ref, corner_ref, out_ref
):
    grid_row, grid_col = place[0], place[1]
    inverse = wide_inverse(factor_ref[...])
    result = dot(inner(inverse, corner_ref[...]), inverse)
    width = rj_ref.shape[1]
    weights = jnp.concatenate([inverse.T, -0.5 * result], axis=1)
    r_own, h_own = rj_ref[...], hj_ref[...]
    z_own = dot(weights, jnp.concatenate([h_own, r_own], axis=0))
    right = jnp.concatenate([z_own, r_own], axis=0)
    lane = lax.broadcasted_iota(jnp.int32, (BLOCK, width), 1)
    inside = (lane >= BLOCK) | (grid_col >= 2)
    parity = lax.rem(grid_col, 2)
    for order, (r_piece, h_piece) in enumerate(((ra_ref, ha_ref), (rb_ref, hb_ref))):
        r_rows = r_piece[...]
        z_rows = dot(weights, jnp.concatenate([h_piece[...], r_rows], axis=0))
        change = inner(jnp.concatenate([r_rows, z_rows], axis=0), right)
        section = parity if order == 0 else 1 - parity
        for m in range(width // BLOCK):
            rows = pl.ds(pl.multiple_of((2 * m + section) * BLOCK, BLOCK), BLOCK)
            part = change[m * BLOCK : (m + 1) * BLOCK]
            out_ref[rows, :] = h_ref[rows, :] - jnp.where(inside, part, 0.0)

    @pl.when(grid_row < 2)
    def _():
        pending = z_own - 0.5 * dot(result, r_own)
        old = h_ref[:BLOCK, :]
        first = grid_row == 0
        rest = jnp.where(first, pending[:BLOCK], pending[BLOCK:])
        lead = jnp.where(first, result[:BLOCK], result[BLOCK:])
        spread = jnp.concatenate([lead] * (width // WIDE), axis=1)
        turned = jnp.concatenate([lead[:, BLOCK:], lead[:, :BLOCK]] * (width // WIDE), axis=1)
        at_zero = jnp.where(first, spread, old)
        head = jnp.where(grid_col == 0, at_zero, turned)
        out_ref[:BLOCK, :] = jnp.where(inside, rest, head)


def finish(place, *operands):
    hamiltonian = operands[0]
    vmem = pl.BlockSpec(memory_space=pltpu.VMEM)
    return pl.pallas_call(
        body,
        out_shape=jax.ShapeDtypeStruct(hamiltonian.shape, jnp.float32),
        in_specs=[pl.BlockSpec(memory_space=pltpu.SMEM)] + [vmem] * len(operands),
        out_specs=vmem,
        compiler_params=pltpu.CompilerParams(vmem_limit_bytes=40 * 1024 * 1024),
        cost_estimate=pl.CostEstimate(flops=10**9, bytes_accessed=5 * 10**6, transcendentals=0),
    )(place, *operands)


def exchange(payload, axis):
    return lax.all_to_all(payload, axis, 0, 0)


def offer(payload, axis, count):
    return exchange(jnp.broadcast_to(payload[None], (count, *payload.shape)), axis)


def per_device(hamiltonian, factor_rows):
    grid_rows, grid_cols = lax.axis_size("row"), lax.axis_size("col")
    row_index, col_index = lax.axis_index("row"), lax.axis_index("col")
    width = hamiltonian.shape[1]
    slab = BLOCK // grid_rows

    def turn(payload):
        direct, crossed = [], []
        for r in range(grid_rows):
            for c in range(grid_cols):
                source = r * grid_cols + c
                row, section = c % grid_rows, c // grid_rows
                direct.append((source, row * grid_cols + 2 * r + section))
                crossed.append((source, row * grid_cols + 2 * r + 1 - section))
        axes = ("row", "col")
        return lax.ppermute(payload, axes, direct), lax.ppermute(payload, axes, crossed)

    ra, rb = turn(factor_rows)
    top = hamiltonian[:BLOCK].reshape(grid_rows, slab, width)
    mine = exchange(top, "row")[:2]
    panel = offer(mine, "row", grid_rows)
    panel = panel.transpose(1, 0, 2, 3).reshape(WIDE, width)
    lead = factor_rows[:, :BLOCK].reshape(2, grid_rows, slab, BLOCK)
    lead = lax.dynamic_index_in_dim(lead, row_index, 1, keepdims=False)
    pieces = offer(jnp.stack([lead, mine[:, :, :BLOCK]]), "col", grid_cols)[:2]
    pieces = offer(pieces, "row", grid_rows)
    pieces = pieces.transpose(2, 3, 0, 4, 1, 5).reshape(2, WIDE, WIDE)
    ha, hb = turn(panel)
    place = jnp.stack([row_index, col_index])
    return finish(
        place, hamiltonian, factor_rows, panel, ra, rb, ha, hb, pieces[0], pieces[1]
    )


def solution(mesh):
    placed = (P("row", "col"), P(None, "col"))
    return jax.shard_map(
        per_device, mesh=mesh, in_specs=placed, out_specs=P("row", "col"), check_vma=False
    )
```

```python
import jax
import jax.numpy as jnp
from jax import lax
from jax.experimental import pallas as pl
from jax.experimental.pallas import tpu as pltpu
from jax.sharding import PartitionSpec as P

BLOCK = 64
WIDE = 2 * BLOCK
EXACT = lax.Precision.HIGHEST


def dot(left, right):
    return jnp.dot(left, right, precision=EXACT, preferred_element_type=jnp.float32)


def inner(left, right):
    return lax.dot_general(
        left, right, (((0,), (0,)), ((), ())), precision=EXACT, preferred_element_type=jnp.float32
    )


def wide_inverse(factor):
    row = lax.broadcasted_iota(jnp.int32, (WIDE, WIDE), 0)
    col = lax.broadcasted_iota(jnp.int32, (WIDE, WIDE), 1)
    on_diag = jnp.where(row == col, factor, 0.0)
    diag_col = jnp.sum(on_diag, axis=1, keepdims=True)
    diag_row = jnp.sum(on_diag, axis=0, keepdims=True)
    same = (row < BLOCK) == (col < BLOCK)
    power = jnp.where((row < col) & same, -factor / diag_col, 0.0)
    total = jnp.where(row == col, 1.0, power)
    for _ in range(5):
        power = dot(power, power)
        total = total + dot(total, power)
    total = total / diag_row
    couple = jnp.where((row < BLOCK) & (col >= BLOCK), factor, 0.0)
    return total - dot(total, dot(couple, total))


def body(place, h_ref, rj_ref, hj_ref, turned_ref, corner_ref, out_ref):
    grid_row, grid_col = place[0], place[1]
    corners = [corner_ref[:, part].reshape(WIDE, WIDE) for part in (0, 1)]
    corner = jnp.concatenate([piece[:, :BLOCK] for piece in corners], axis=1)
    inverse = wide_inverse(jnp.concatenate([piece[:, BLOCK:] for piece in corners], axis=1))
    result = dot(inner(inverse, corner), inverse)
    width = rj_ref.shape[1]
    r_own, h_own = rj_ref[...], hj_ref[...]
    weights = jnp.concatenate([inverse.T, -0.5 * result], axis=1)
    z_own = dot(weights, jnp.concatenate([h_own, r_own], axis=0))
    right = jnp.concatenate([z_own, r_own], axis=0)
    across = jnp.concatenate([-0.5 * result.T, inverse], axis=0)
    holders, twice, _ = turned_ref.shape
    slab = twice // 2
    r_pieces = turned_ref[:, :slab].reshape(2, WIDE, width)
    h_rows = jnp.concatenate(
        [
            turned_ref[:, slab:, part * WIDE : (part + 1) * WIDE].reshape(holders, 1, slab, WIDE)
            for part in range(width // WIDE)
        ],
        axis=1,
    ).reshape(-1, WIDE)
    lane = lax.broadcasted_iota(jnp.int32, (BLOCK, width), 1)
    inside = (lane >= BLOCK) | (grid_col >= 2)
    for section in range(2):
        r_cols = r_pieces[section].T
        h_cols = jnp.concatenate(
            [
                h_rows[(2 * m + section) * BLOCK : (2 * m + section + 1) * BLOCK]
                for m in range(width // BLOCK)
            ],
            axis=0,
        )
        z_cols = dot(jnp.concatenate([r_cols, h_cols], axis=1), across)
        change = dot(jnp.concatenate([r_cols, z_cols], axis=1), right)
        for m in range(width // BLOCK):
            rows = slice((2 * m + section) * BLOCK, (2 * m + section + 1) * BLOCK)
            part = change[m * BLOCK : (m + 1) * BLOCK]
            out_ref[rows, :] = h_ref[rows, :] - jnp.where(inside, part, 0.0)

    @pl.when(grid_row < 2)
    def _():
        pending = z_own - 0.5 * dot(result, r_own)
        old = h_ref[:BLOCK, :]
        first = grid_row == 0
        rest = jnp.where(first, pending[:BLOCK], pending[BLOCK:])
        lead = jnp.where(first, result[:BLOCK], result[BLOCK:])
        spread = jnp.concatenate([lead] * (width // WIDE), axis=1)
        turned = jnp.concatenate([lead[:, BLOCK:], lead[:, :BLOCK]] * (width // WIDE), axis=1)
        at_zero = jnp.where(first, spread, old)
        head = jnp.where(grid_col == 0, at_zero, turned)
        out_ref[:BLOCK, :] = jnp.where(inside, rest, head)


def finish(place, *operands):
    hamiltonian = operands[0]
    vmem = pl.BlockSpec(memory_space=pltpu.VMEM)
    return pl.pallas_call(
        body,
        out_shape=jax.ShapeDtypeStruct(hamiltonian.shape, jnp.float32),
        in_specs=[pl.BlockSpec(memory_space=pltpu.SMEM)] + [vmem] * len(operands),
        out_specs=vmem,
        compiler_params=pltpu.CompilerParams(vmem_limit_bytes=40 * 1024 * 1024),
        cost_estimate=pl.CostEstimate(flops=10**9, bytes_accessed=5 * 10**6, transcendentals=0),
    )(place, *operands)


def exchange(payload, axis):
    return lax.all_to_all(payload, axis, 0, 0)


def offer(payload, axis, count):
    return exchange(jnp.broadcast_to(payload[None], (count, *payload.shape)), axis)


def per_device(hamiltonian, factor_rows):
    grid_rows, grid_cols = lax.axis_size("row"), lax.axis_size("col")
    row_index, col_index = lax.axis_index("row"), lax.axis_index("col")
    height, width = hamiltonian.shape
    slab = WIDE // grid_rows

    top = hamiltonian[:BLOCK].reshape(grid_rows // 2, slab, width)
    top = exchange(jnp.concatenate([top, top]), "row")
    h_slab = jnp.where(row_index < grid_rows // 2, top[0], top[1])
    side = hamiltonian[:, :BLOCK].reshape(grid_cols, height // grid_cols, BLOCK)
    side = exchange(side, "col")
    h_share = jnp.concatenate([side[0], side[1]], axis=1)
    h_share = h_share.reshape(width // WIDE, slab, WIDE)
    r_slab = lax.dynamic_slice_in_dim(factor_rows, row_index * slab, slab, 0)
    pairs = [
        (r * grid_cols + c, (c % grid_rows) * grid_cols + grid_rows * (c // grid_rows) + r)
        for r in range(grid_rows)
        for c in range(grid_cols)
    ]
    r_share = lax.ppermute(r_slab, ("row", "col"), pairs)

    corner = jnp.concatenate([h_slab[:, :BLOCK], r_slab[:, :BLOCK]], axis=1)
    corner = offer(corner, "col", grid_cols)[:2]
    panel = offer(h_slab, "row", grid_rows).reshape(WIDE, width)
    share = jnp.concatenate([r_share, jnp.concatenate(list(h_share), axis=1)], axis=0)
    turned = lax.all_gather(share, "col")
    corner = offer(corner, "row", grid_rows)
    place = jnp.stack([row_index, col_index])
    return finish(place, hamiltonian, factor_rows, panel, turned, corner)


def solution(mesh):
    placed = (P("row", "col"), P(None, "col"))
    return jax.shard_map(
        per_device, mesh=mesh, in_specs=placed, out_specs=P("row", "col"), check_vma=False
    )
```

```python
import jax
import jax.numpy as jnp
from jax import lax
from jax.experimental import pallas as pl
from jax.experimental.pallas import tpu as pltpu
from jax.sharding import PartitionSpec as P

BLOCK = 64
WIDE = 2 * BLOCK
EXACT = lax.Precision.HIGHEST


def dot(left, right):
    return jnp.dot(left, right, precision=EXACT, preferred_element_type=jnp.float32)


def inner(left, right):
    return lax.dot_general(
        left, right, (((0,), (0,)), ((), ())), precision=EXACT, preferred_element_type=jnp.float32
    )


def wide_inverse(factor):
    row = lax.broadcasted_iota(jnp.int32, (WIDE, WIDE), 0)
    col = lax.broadcasted_iota(jnp.int32, (WIDE, WIDE), 1)
    on_diag = jnp.where(row == col, factor, 0.0)
    diag_col = jnp.sum(on_diag, axis=1, keepdims=True)
    diag_row = jnp.sum(on_diag, axis=0, keepdims=True)
    same = (row < BLOCK) == (col < BLOCK)
    power = jnp.where((row < col) & same, -factor / diag_col, 0.0)
    total = jnp.where(row == col, 1.0, power)
    for _ in range(5):
        power = dot(power, power)
        total = total + dot(total, power)
    total = total / diag_row
    couple = jnp.where((row < BLOCK) & (col >= BLOCK), factor, 0.0)
    return total - dot(total, dot(couple, total))


def beside(left, right):
    return jnp.concatenate([left, right], axis=1)


def owner_of(block):
    k = block // 4
    return (block + k) % 4, k


def pack_columns(h_ref, r_ref, out_ref):
    h_cols, r_cols = h_ref[:, :BLOCK], r_ref[:, :BLOCK]
    first = h_cols[: 4 * BLOCK]
    second = jnp.concatenate([h_cols[7 * BLOCK : 8 * BLOCK], h_cols[4 * BLOCK : 7 * BLOCK]])
    third = jnp.concatenate([h_cols[10 * BLOCK :], h_cols[8 * BLOCK : 10 * BLOCK]])
    corner = jnp.concatenate([h_cols[:BLOCK], h_cols[:BLOCK], r_cols])
    out_ref[:, 0] = beside(first, second).reshape(-1, 8, WIDE)
    out_ref[:, 1] = beside(third, corner).reshape(-1, 8, WIDE)


def pack_share(halves_ref, out_ref):
    for slot in range(2):
        left, right = halves_ref[0, slot], halves_ref[1, slot]
        low = beside(left[:, :BLOCK], right[:, :BLOCK])
        high = beside(left[:, BLOCK:], right[:, BLOCK:])
        for row in range(out_ref.shape[0]):
            out_ref[row, 2 * slot] = low
            out_ref[row, 2 * slot + 1] = high


def pack_gather(place, all_ref, r_ref, out_ref):
    grid_row, grid_col = place[0], place[1]
    grid_rows, grid_cols = all_ref.shape[0], out_ref.shape[0]
    own = all_ref[grid_row]
    corner_from = jnp.minimum(grid_col // 8, 1)
    corner = all_ref[corner_from, 3]
    parity = lax.rem(grid_col // 8, 2)
    for col in range(grid_cols):
        section = col // grid_rows
        lead = jnp.where(parity == section, 0, 1)
        for k in range(3):
            out_ref[col, k] = own[k]
        out_ref[col, 3] = all_ref[col % grid_rows, lead]
        out_ref[col, 4] = all_ref[col % grid_rows, 2]
        out_ref[col, 5] = corner
        for k in range(3):
            out_ref[col, 6 + k] = r_ref[:, k * WIDE : (k + 1) * WIDE]


def body(place, h_ref, rj_ref, got_ref, out_ref):
    grid_row, grid_col = place[0], place[1]
    width = rj_ref.shape[1]
    corner = got_ref[:, 5].reshape(2, WIDE, WIDE)
    inverse = wide_inverse(corner[1])
    result = dot(inner(inverse, corner[0]), inverse)
    own_section = grid_col // 16
    h_own = []
    for m in range(width // BLOCK):
        (even, k), (odd, _) = owner_of(2 * m), owner_of(2 * m + 1)
        group = jnp.where(own_section == 0, even, odd)
        slot = 4 if k == 2 else 3
        h_own.append(got_ref[pl.ds(8 * group, 8), slot].reshape(BLOCK, WIDE))
    h_own = jnp.concatenate(h_own).T
    r_own = rj_ref[...]
    weights = beside(inverse.T, -0.5 * result)
    z_own = dot(weights, jnp.concatenate([h_own, r_own], axis=0))
    right = jnp.concatenate([z_own, r_own], axis=0)
    across = jnp.concatenate([-0.5 * result.T, inverse], axis=0)
    lane = lax.broadcasted_iota(jnp.int32, (BLOCK, width), 1)
    inside = (lane >= BLOCK) | (grid_col >= 2)
    for section in range(2):
        r_piece = jnp.concatenate(
            [
                got_ref[16 * section : 16 * section + 16, 6 + k].reshape(WIDE, WIDE).T
                for k in range(width // WIDE)
            ]
        )
        h_piece = []
        for m in range(width // BLOCK):
            group, k = owner_of(2 * m + section)
            h_piece.append(got_ref[8 * group : 8 * group + 8, k].reshape(BLOCK, WIDE))
        z_piece = dot(beside(r_piece, jnp.concatenate(h_piece)), across)
        change = dot(beside(r_piece, z_piece), right)
        for m in range(width // BLOCK):
            rows = slice((2 * m + section) * BLOCK, (2 * m + section + 1) * BLOCK)
            part = change[m * BLOCK : (m + 1) * BLOCK]
            out_ref[rows, :] = h_ref[rows, :] - jnp.where(inside, part, 0.0)

    @pl.when(grid_row < 2)
    def _():
        pending = z_own - 0.5 * dot(result, r_own)
        old = h_ref[:BLOCK, :]
        first = grid_row == 0
        rest = jnp.where(first, pending[:BLOCK], pending[BLOCK:])
        lead = jnp.where(first, result[:BLOCK], result[BLOCK:])
        spread = jnp.concatenate([lead] * (width // WIDE), axis=1)
        turned = jnp.concatenate([beside(lead[:, BLOCK:], lead[:, :BLOCK])] * (width // WIDE), axis=1)
        at_zero = jnp.where(first, spread, old)
        head = jnp.where(grid_col == 0, at_zero, turned)
        out_ref[:BLOCK, :] = jnp.where(inside, rest, head)


VMEM = pl.BlockSpec(memory_space=pltpu.VMEM)
SMEM = pl.BlockSpec(memory_space=pltpu.SMEM)


def call(function, shape, specs, *operands, **more):
    return pl.pallas_call(
        function,
        out_shape=jax.ShapeDtypeStruct(shape, jnp.float32),
        in_specs=specs,
        out_specs=VMEM,
        compiler_params=pltpu.CompilerParams(vmem_limit_bytes=40 * 1024 * 1024),
        **more,
    )(*operands)


def exchange(payload, axis):
    return lax.all_to_all(payload, axis, 0, 0)


def per_device(hamiltonian, factor_rows):
    grid_rows, grid_cols = lax.axis_size("row"), lax.axis_size("col")
    row_index, col_index = lax.axis_index("row"), lax.axis_index("col")
    place = jnp.stack([row_index, col_index])

    slab = WIDE // grid_rows
    pairs = [
        (r * grid_cols + c, (c % grid_rows) * grid_cols + grid_rows * (c // grid_rows) + r)
        for r in range(grid_rows)
        for c in range(grid_cols)
    ]
    r_slab = lax.dynamic_slice_in_dim(factor_rows, row_index * slab, slab, 0)
    r_share = lax.ppermute(r_slab, ("row", "col"), pairs)

    halves = call(
        pack_columns,
        (grid_cols, 2, 8, WIDE),
        [VMEM, VMEM],
        hamiltonian[:, :WIDE],
        factor_rows[:, :WIDE],
    )
    halves = exchange(halves, "col")
    share = call(pack_share, (grid_rows, 4, 8, WIDE), [VMEM], halves[:2])
    shares = exchange(share, "row")
    offer = call(pack_gather, (grid_cols, 9, 8, WIDE), [SMEM, VMEM, VMEM], place, shares, r_share)
    got = exchange(offer, "col")
    cost = pl.CostEstimate(flops=10**9, bytes_accessed=5 * 10**6, transcendentals=0)
    return call(
        body,
        hamiltonian.shape,
        [SMEM, VMEM, VMEM, VMEM],
        place,
        hamiltonian,
        factor_rows,
        got,
        cost_estimate=cost,
    )


def solution(mesh):
    placed = (P("row", "col"), P(None, "col"))
    return jax.shard_map(
        per_device, mesh=mesh, in_specs=placed, out_specs=P("row", "col"), check_vma=False
    )
```

```python
import jax
import jax.numpy as jnp
from jax import lax
from jax.experimental import pallas as pl
from jax.experimental.pallas import tpu as pltpu
from jax.sharding import PartitionSpec as P

BLOCK = 64
WIDE = 2 * BLOCK
EXACT = lax.Precision.HIGHEST


def dot(left, right):
    return jnp.dot(left, right, precision=EXACT, preferred_element_type=jnp.float32)


def inner(left, right):
    return lax.dot_general(
        left, right, (((0,), (0,)), ((), ())), precision=EXACT, preferred_element_type=jnp.float32
    )


def wide_inverse(factor):
    row = lax.broadcasted_iota(jnp.int32, (WIDE, WIDE), 0)
    col = lax.broadcasted_iota(jnp.int32, (WIDE, WIDE), 1)
    on_diag = jnp.where(row == col, factor, 0.0)
    diag_col = jnp.sum(on_diag, axis=1, keepdims=True)
    diag_row = jnp.sum(on_diag, axis=0, keepdims=True)
    same = (row < BLOCK) == (col < BLOCK)
    power = jnp.where((row < col) & same, -factor / diag_col, 0.0)
    total = jnp.where(row == col, 1.0, power)
    power = dot(power, power)
    for _ in range(4):
        both = dot(jnp.concatenate([power, total], axis=0), power)
        power, total = both[:WIDE], total + both[WIDE:]
    total = (total + dot(total, power)) / diag_row
    couple = jnp.where((row < BLOCK) & (col >= BLOCK), factor, 0.0)
    return total - dot(total, dot(couple, total))


def beside(left, right):
    return jnp.concatenate([left, right], axis=1)


def owner_of(block):
    k = block // 4
    return (block + k) % 4, k


def pack_columns(h_ref, r_ref, out_ref):
    h_cols, r_cols = h_ref[:, :BLOCK], r_ref[:, :BLOCK]
    first = h_cols[: 4 * BLOCK]
    second = jnp.concatenate([h_cols[7 * BLOCK : 8 * BLOCK], h_cols[4 * BLOCK : 7 * BLOCK]])
    third = jnp.concatenate([h_cols[10 * BLOCK :], h_cols[8 * BLOCK : 10 * BLOCK]])
    corner = jnp.concatenate([h_cols[:BLOCK], h_cols[:BLOCK], r_cols])
    out_ref[:, 0] = beside(first, second).reshape(-1, 8, WIDE)
    out_ref[:, 1] = beside(third, corner).reshape(-1, 8, WIDE)


def pack_share(halves_ref, out_ref):
    for slot in range(2):
        left, right = halves_ref[0, slot], halves_ref[1, slot]
        low = beside(left[:, :BLOCK], right[:, :BLOCK])
        high = beside(left[:, BLOCK:], right[:, BLOCK:])
        for row in range(out_ref.shape[0]):
            out_ref[row, 2 * slot] = low
            out_ref[row, 2 * slot + 1] = high


def pack_gather(place, all_ref, out_ref):
    grid_row, grid_col = place[0], place[1]
    grid_rows, grid_cols = all_ref.shape[0], out_ref.shape[0]
    own = all_ref[grid_row]
    corner_from = jnp.minimum(grid_col // 8, 1)
    corner = all_ref[corner_from, 3]
    parity = lax.rem(grid_col // 8, 2)
    for col in range(grid_cols):
        section = col // grid_rows
        lead = jnp.where(parity == section, 0, 1)
        for k in range(3):
            out_ref[col, k] = own[k]
        out_ref[col, 3] = all_ref[col % grid_rows, lead]
        out_ref[col, 4] = all_ref[col % grid_rows, 2]
        out_ref[col, 5] = corner


def body(place, h_ref, rj_ref, got_ref, ra_ref, rb_ref, out_ref):
    grid_row, grid_col = place[0], place[1]
    width = rj_ref.shape[1]
    corner = got_ref[:, 5].reshape(2, WIDE, WIDE)
    inverse = wide_inverse(corner[1])
    result = dot(inner(inverse, corner[0]), inverse)
    own_section = grid_col // 16
    h_own = []
    for m in range(width // BLOCK):
        (even, k), (odd, _) = owner_of(2 * m), owner_of(2 * m + 1)
        group = jnp.where(own_section == 0, even, odd)
        slot = 4 if k == 2 else 3
        h_own.append(got_ref[pl.ds(8 * group, 8), slot].reshape(BLOCK, WIDE))
    h_own = jnp.concatenate(h_own).T
    r_own = rj_ref[...]
    weights = beside(inverse.T, -0.5 * result)
    z_own = dot(weights, jnp.concatenate([h_own, r_own], axis=0))
    right = jnp.concatenate([z_own, r_own], axis=0)
    across = jnp.concatenate([-0.5 * result.T, inverse], axis=0)
    lane = lax.broadcasted_iota(jnp.int32, (BLOCK, width), 1)
    inside = (lane >= BLOCK) | (grid_col >= 2)
    straight = lax.rem(grid_col // 8, 2) == 0
    for section in range(2):
        r_piece = jnp.where(straight == (section == 0), ra_ref[...], rb_ref[...]).T
        h_piece = []
        for m in range(width // BLOCK):
            group, k = owner_of(2 * m + section)
            h_piece.append(got_ref[8 * group : 8 * group + 8, k].reshape(BLOCK, WIDE))
        z_piece = dot(beside(r_piece, jnp.concatenate(h_piece)), across)
        change = dot(beside(r_piece, z_piece), right)
        for m in range(width // BLOCK):
            rows = slice((2 * m + section) * BLOCK, (2 * m + section + 1) * BLOCK)
            part = change[m * BLOCK : (m + 1) * BLOCK]
            out_ref[rows, :] = h_ref[rows, :] - jnp.where(inside, part, 0.0)

    @pl.when(grid_row < 2)
    def _():
        pending = z_own - 0.5 * dot(result, r_own)
        old = h_ref[:BLOCK, :]
        first = grid_row == 0
        rest = jnp.where(first, pending[:BLOCK], pending[BLOCK:])
        lead = jnp.where(first, result[:BLOCK], result[BLOCK:])
        spread = jnp.concatenate([lead] * (width // WIDE), axis=1)
        turned = jnp.concatenate([beside(lead[:, BLOCK:], lead[:, :BLOCK])] * (width // WIDE), axis=1)
        at_zero = jnp.where(first, spread, old)
        head = jnp.where(grid_col == 0, at_zero, turned)
        out_ref[:BLOCK, :] = jnp.where(inside, rest, head)


VMEM = pl.BlockSpec(memory_space=pltpu.VMEM)
SMEM = pl.BlockSpec(memory_space=pltpu.SMEM)


def call(function, shape, specs, *operands, **more):
    return pl.pallas_call(
        function,
        out_shape=jax.ShapeDtypeStruct(shape, jnp.float32),
        in_specs=specs,
        out_specs=VMEM,
        compiler_params=pltpu.CompilerParams(vmem_limit_bytes=40 * 1024 * 1024),
        **more,
    )(*operands)


def exchange(payload, axis):
    return lax.all_to_all(payload, axis, 0, 0)


def per_device(hamiltonian, factor_rows):
    grid_rows, grid_cols = lax.axis_size("row"), lax.axis_size("col")
    row_index, col_index = lax.axis_index("row"), lax.axis_index("col")
    place = jnp.stack([row_index, col_index])

    moves = ([], [])
    for r in range(grid_rows):
        for c in range(grid_cols):
            section = c // grid_rows
            for turn in range(2):
                pick = 2 * (r % 2) + turn
                x, y = pick ^ section, (c + r // 2 + 2 * pick) % 8
                moves[turn].append((r * grid_cols + c, (c % grid_rows) * grid_cols + 8 * x + y))
    r_pieces = [lax.ppermute(factor_rows, ("row", "col"), pairs) for pairs in moves]

    halves = call(
        pack_columns,
        (grid_cols, 2, 8, WIDE),
        [pl.BlockSpec((rows, WIDE), lambda i: (0, 0)) for rows in (hamiltonian.shape[0], WIDE)],
        hamiltonian,
        factor_rows,
        grid=(1,),
    )
    halves = exchange(halves, "col")
    halves, r_first = lax.optimization_barrier((halves, r_pieces[0]))
    share = call(pack_share, (grid_rows, 4, 8, WIDE), [VMEM], halves[:2])
    shares = exchange(share, "row")
    shares, r_second = lax.optimization_barrier((shares, r_pieces[1]))
    offer = call(pack_gather, (grid_cols, 6, 8, WIDE), [SMEM, VMEM], place, shares)
    got = exchange(offer, "col")
    cost = pl.CostEstimate(flops=10**9, bytes_accessed=5 * 10**6, transcendentals=0)
    return call(
        body,
        hamiltonian.shape,
        [SMEM] + [VMEM] * 5,
        place,
        hamiltonian,
        factor_rows,
        got,
        r_first,
        r_second,
        cost_estimate=cost,
    )


def solution(mesh):
    placed = (P("row", "col"), P(None, "col"))
    return jax.shard_map(
        per_device, mesh=mesh, in_specs=placed, out_specs=P("row", "col"), check_vma=False
    )
```

```python
import jax
import jax.numpy as jnp
from jax import lax
from jax.experimental import pallas as pl
from jax.experimental.pallas import tpu as pltpu
from jax.sharding import PartitionSpec as P

BLOCK = 64
WIDE = 2 * BLOCK
EXACT = lax.Precision.HIGHEST


def dot(left, right):
    return jnp.dot(left, right, precision=EXACT, preferred_element_type=jnp.float32)


def inner(left, right):
    return lax.dot_general(
        left, right, (((0,), (0,)), ((), ())), precision=EXACT, preferred_element_type=jnp.float32
    )


def wide_inverse(factor):
    row = lax.broadcasted_iota(jnp.int32, (WIDE, WIDE), 0)
    col = lax.broadcasted_iota(jnp.int32, (WIDE, WIDE), 1)
    on_diag = jnp.where(row == col, factor, 0.0)
    diag_col = jnp.sum(on_diag, axis=1, keepdims=True)
    diag_row = jnp.sum(on_diag, axis=0, keepdims=True)
    same = (row < BLOCK) == (col < BLOCK)
    power = jnp.where((row < col) & same, -factor / diag_col, 0.0)
    total = jnp.where(row == col, 1.0, power)
    power = dot(power, power)
    for _ in range(4):
        both = dot(jnp.concatenate([power, total], axis=0), power)
        power, total = both[:WIDE], total + both[WIDE:]
    total = (total + dot(total, power)) / diag_row
    couple = jnp.where((row < BLOCK) & (col >= BLOCK), factor, 0.0)
    return total - dot(total, dot(couple, total))


def beside(*parts):
    return jnp.concatenate(parts, axis=1)


def double_top(h_ref, out_ref, sems):
    copies = [
        pltpu.make_async_copy(
            h_ref.at[pl.ds(0, BLOCK)], out_ref.at[pl.ds(half * BLOCK, BLOCK)], sems.at[half]
        )
        for half in range(2)
    ]
    for copy in copies:
        copy.start()
    for copy in copies:
        copy.wait()


def pack_slab(place, slabs_ref, share_ref, slab_ref, out_ref):
    first = place[0] < slabs_ref.shape[0] // 2
    h_slab = jnp.where(first, slabs_ref[0], slabs_ref[1])
    packed = beside(h_slab, share_ref[...], slab_ref[:, :WIDE])
    for col in range(out_ref.shape[0]):
        out_ref[col] = packed


def pack_rows(place, slabs_ref, all_ref, out_ref):
    grid_rows, width = slabs_ref.shape[0], slabs_ref.shape[2]
    first = place[0] < grid_rows // 2
    own = jnp.where(first, slabs_ref[0], slabs_ref[1])
    left, right = all_ref[0], all_ref[1]
    tail = beside(
        own,
        left[:, :BLOCK],
        right[:, :BLOCK],
        left[:, 2 * width : 2 * width + BLOCK],
        right[:, 2 * width : 2 * width + BLOCK],
    )
    for row in range(grid_rows):
        out_ref[row, :, :width] = all_ref[row, :, :width]
        out_ref[row, :, width : 2 * width] = all_ref[row + grid_rows, :, :width]
        out_ref[row, :, 2 * width :] = tail


def body(place, h_ref, rj_ref, got_ref, all_ref, out_ref):
    grid_row, grid_col = place[0], place[1]
    width = rj_ref.shape[1]
    inverse = wide_inverse(got_ref[:, 3 * width + WIDE :])
    result = dot(inner(inverse, got_ref[:, 3 * width : 3 * width + WIDE]), inverse)
    weights = beside(inverse.T, -0.5 * result)
    r_own = rj_ref[...]
    z_own = dot(weights, jnp.concatenate([got_ref[:, 2 * width : 3 * width], r_own]))
    right = jnp.concatenate([z_own, r_own])
    lane = lax.broadcasted_iota(jnp.int32, (BLOCK, width), 1)
    inside = (lane >= BLOCK) | (grid_col >= 2)
    holders = all_ref.shape[0] // 2
    for section in range(2):
        r_rows = all_ref[section * holders : (section + 1) * holders, :, width : 2 * width]
        r_rows = r_rows.reshape(WIDE, width)
        h_rows = got_ref[:, section * width : (section + 1) * width]
        z_rows = dot(weights, jnp.concatenate([h_rows, r_rows]))
        change = inner(jnp.concatenate([r_rows, z_rows]), right)
        for m in range(width // BLOCK):
            rows = slice((2 * m + section) * BLOCK, (2 * m + section + 1) * BLOCK)
            part = change[m * BLOCK : (m + 1) * BLOCK]
            out_ref[rows, :] = h_ref[rows, :] - jnp.where(inside, part, 0.0)

    @pl.when(grid_row < 2)
    def _():
        pending = z_own - 0.5 * dot(result, r_own)
        old = h_ref[:BLOCK, :]
        first = grid_row == 0
        rest = jnp.where(first, pending[:BLOCK], pending[BLOCK:])
        lead = jnp.where(first, result[:BLOCK], result[BLOCK:])
        spread = beside(*[lead] * (width // WIDE))
        turned = beside(*[lead[:, BLOCK:], lead[:, :BLOCK]] * (width // WIDE))
        at_zero = jnp.where(first, spread, old)
        head = jnp.where(grid_col == 0, at_zero, turned)
        out_ref[:BLOCK, :] = jnp.where(inside, rest, head)


VMEM = pl.BlockSpec(memory_space=pltpu.VMEM)
SMEM = pl.BlockSpec(memory_space=pltpu.SMEM)


def call(function, shape, specs, *operands, **more):
    return pl.pallas_call(
        function,
        out_shape=jax.ShapeDtypeStruct(shape, jnp.float32),
        in_specs=specs,
        out_specs=VMEM,
        compiler_params=pltpu.CompilerParams(vmem_limit_bytes=40 * 1024 * 1024),
        **more,
    )(*operands)


def exchange(payload, axis):
    return lax.all_to_all(payload, axis, 0, 0)


def per_device(hamiltonian, factor_rows):
    grid_rows, grid_cols = lax.axis_size("row"), lax.axis_size("col")
    row_index, col_index = lax.axis_index("row"), lax.axis_index("col")
    place = jnp.stack([row_index, col_index])
    width = hamiltonian.shape[1]
    slab = WIDE // grid_rows

    pairs = [
        (r * grid_cols + c, (c % grid_rows) * grid_cols + grid_rows * (c // grid_rows) + r)
        for r in range(grid_rows)
        for c in range(grid_cols)
    ]
    r_slab = lax.dynamic_slice_in_dim(factor_rows, row_index * slab, slab, 0)
    r_share = lax.ppermute(r_slab, ("row", "col"), pairs)

    top = call(
        double_top,
        (WIDE, width),
        [pl.BlockSpec(memory_space=pl.ANY)],
        hamiltonian,
        scratch_shapes=[pltpu.SemaphoreType.DMA((2,))],
    )
    slabs = exchange(top.reshape(grid_rows, slab, width), "row")
    shape = (grid_cols, slab, 2 * width + WIDE)
    everything = call(
        pack_slab, shape, [SMEM, VMEM, VMEM, VMEM], place, slabs, r_share, r_slab
    )
    everything = exchange(everything, "col")
    shape = (grid_rows, slab, 3 * width + 2 * WIDE)
    got = call(pack_rows, shape, [SMEM, VMEM, VMEM], place, slabs, everything)
    got = exchange(got, "row").reshape(WIDE, -1)
    cost = pl.CostEstimate(flops=10**9, bytes_accessed=5 * 10**6, transcendentals=0)
    return call(
        body,
        hamiltonian.shape,
        [SMEM] + [VMEM] * 4,
        place,
        hamiltonian,
        factor_rows,
        got,
        everything,
        cost_estimate=cost,
    )


def solution(mesh):
    placed = (P("row", "col"), P(None, "col"))
    return jax.shard_map(
        per_device, mesh=mesh, in_specs=placed, out_specs=P("row", "col"), check_vma=False
    )
```

```python
import jax
import jax.numpy as jnp
from jax import lax
from jax.experimental import pallas as pl
from jax.experimental.pallas import tpu as pltpu
from jax.sharding import PartitionSpec as P

BLOCK = 64
WIDE = 2 * BLOCK
EXACT = lax.Precision.HIGHEST


def dot(left, right):
    return jnp.dot(left, right, precision=EXACT, preferred_element_type=jnp.float32)


def inner(left, right):
    return lax.dot_general(
        left, right, (((0,), (0,)), ((), ())), precision=EXACT, preferred_element_type=jnp.float32
    )


def wide_inverse(factor):
    row = lax.broadcasted_iota(jnp.int32, (WIDE, WIDE), 0)
    col = lax.broadcasted_iota(jnp.int32, (WIDE, WIDE), 1)
    on_diag = jnp.where(row == col, factor, 0.0)
    diag_col = jnp.sum(on_diag, axis=1, keepdims=True)
    diag_row = jnp.sum(on_diag, axis=0, keepdims=True)
    same = (row < BLOCK) == (col < BLOCK)
    power = jnp.where((row < col) & same, -factor / diag_col, 0.0)
    total = jnp.where(row == col, 1.0, power)
    for _ in range(5):
        power = dot(power, power)
        total = total + dot(total, power)
    total = total / diag_row
    couple = jnp.where((row < BLOCK) & (col >= BLOCK), factor, 0.0)
    return total - dot(total, dot(couple, total))


def beside(left, right):
    return jnp.concatenate([left, right], axis=1)


def owner_of(block):
    k = block // 4
    return (block + k) % 4, k


def pack_columns(h_ref, r_ref, out_ref):
    h_cols, r_cols = h_ref[:, :BLOCK], r_ref[:, :BLOCK]
    first = h_cols[: 4 * BLOCK]
    second = jnp.concatenate([h_cols[7 * BLOCK : 8 * BLOCK], h_cols[4 * BLOCK : 7 * BLOCK]])
    third = jnp.concatenate([h_cols[10 * BLOCK :], h_cols[8 * BLOCK : 10 * BLOCK]])
    corner = jnp.concatenate([h_cols[:BLOCK], h_cols[:BLOCK], r_cols])
    out_ref[:, 0] = beside(first, second).reshape(-1, 8, WIDE)
    out_ref[:, 1] = beside(third, corner).reshape(-1, 8, WIDE)


def pack_share(halves_ref, out_ref):
    for slot in range(2):
        left, right = halves_ref[0, slot], halves_ref[1, slot]
        low = beside(left[:, :BLOCK], right[:, :BLOCK])
        high = beside(left[:, BLOCK:], right[:, BLOCK:])
        for row in range(out_ref.shape[0]):
            out_ref[row, 2 * slot] = low
            out_ref[row, 2 * slot + 1] = high


def pack_gather(place, all_ref, out_ref):
    grid_row, grid_col = place[0], place[1]
    grid_rows, grid_cols = all_ref.shape[0], out_ref.shape[0]
    own = all_ref[grid_row]
    corner_from = jnp.minimum(grid_col // 8, 1)
    corner = all_ref[corner_from, 3]
    parity = lax.rem(grid_col // 8, 2)
    for col in range(grid_cols):
        section = col // grid_rows
        lead = jnp.where(parity == section, 0, 1)
        for k in range(3):
            out_ref[col, k] = own[k]
        out_ref[col, 3] = all_ref[col % grid_rows, lead]
        out_ref[col, 4] = all_ref[col % grid_rows, 2]
        out_ref[col, 5] = corner


def body(place, h_ref, rj_ref, got_ref, r_all_ref, out_ref, r_ref, sem):
    grid_row, grid_col = place[0], place[1]
    width = rj_ref.shape[1]
    fetch = pltpu.make_async_copy(r_all_ref.at[:, pl.ds(0, 8)], r_ref, sem)
    fetch.start()
    corner = got_ref[:, 5].reshape(2, WIDE, WIDE)
    inverse = wide_inverse(corner[1])
    result = dot(inner(inverse, corner[0]), inverse)
    own_section = grid_col // 16
    h_own = []
    for m in range(width // BLOCK):
        (even, k), (odd, _) = owner_of(2 * m), owner_of(2 * m + 1)
        group = jnp.where(own_section == 0, even, odd)
        slot = 4 if k == 2 else 3
        h_own.append(got_ref[pl.ds(8 * group, 8), slot].reshape(BLOCK, WIDE))
    h_own = jnp.concatenate(h_own).T
    r_own = rj_ref[...]
    weights = beside(inverse.T, -0.5 * result)
    z_own = dot(weights, jnp.concatenate([h_own, r_own], axis=0))
    right = jnp.concatenate([z_own, r_own], axis=0)
    across = jnp.concatenate([-0.5 * result.T, inverse], axis=0)
    lane = lax.broadcasted_iota(jnp.int32, (BLOCK, width), 1)
    inside = (lane >= BLOCK) | (grid_col >= 2)
    fetch.wait()
    for section in range(2):
        r_piece = r_ref[16 * section : 16 * section + 16].reshape(WIDE, width).T
        h_piece = []
        for m in range(width // BLOCK):
            group, k = owner_of(2 * m + section)
            h_piece.append(got_ref[8 * group : 8 * group + 8, k].reshape(BLOCK, WIDE))
        z_piece = dot(beside(r_piece, jnp.concatenate(h_piece)), across)
        change = dot(beside(r_piece, z_piece), right)
        for m in range(width // BLOCK):
            rows = slice((2 * m + section) * BLOCK, (2 * m + section + 1) * BLOCK)
            part = change[m * BLOCK : (m + 1) * BLOCK]
            out_ref[rows, :] = h_ref[rows, :] - jnp.where(inside, part, 0.0)

    @pl.when(grid_row < 2)
    def _():
        pending = z_own - 0.5 * dot(result, r_own)
        old = h_ref[:BLOCK, :]
        first = grid_row == 0
        rest = jnp.where(first, pending[:BLOCK], pending[BLOCK:])
        lead = jnp.where(first, result[:BLOCK], result[BLOCK:])
        spread = jnp.concatenate([lead] * (width // WIDE), axis=1)
        turned = jnp.concatenate([beside(lead[:, BLOCK:], lead[:, :BLOCK])] * (width // WIDE), axis=1)
        at_zero = jnp.where(first, spread, old)
        head = jnp.where(grid_col == 0, at_zero, turned)
        out_ref[:BLOCK, :] = jnp.where(inside, rest, head)


VMEM = pl.BlockSpec(memory_space=pltpu.VMEM)
SMEM = pl.BlockSpec(memory_space=pltpu.SMEM)


def call(function, shape, specs, *operands, **more):
    return pl.pallas_call(
        function,
        out_shape=jax.ShapeDtypeStruct(shape, jnp.float32),
        in_specs=specs,
        out_specs=VMEM,
        compiler_params=pltpu.CompilerParams(vmem_limit_bytes=40 * 1024 * 1024),
        **more,
    )(*operands)


def exchange(payload, axis):
    return lax.all_to_all(payload, axis, 0, 0)


def per_device(hamiltonian, factor_rows):
    grid_rows, grid_cols = lax.axis_size("row"), lax.axis_size("col")
    row_index, col_index = lax.axis_index("row"), lax.axis_index("col")
    place = jnp.stack([row_index, col_index])

    slab = WIDE // grid_rows
    pairs = [
        (r * grid_cols + c, (c % grid_rows) * grid_cols + grid_rows * (c // grid_rows) + r)
        for r in range(grid_rows)
        for c in range(grid_cols)
    ]
    r_slab = lax.dynamic_slice_in_dim(factor_rows, row_index * slab, slab, 0)
    r_share = lax.ppermute(r_slab, ("row", "col"), pairs)

    r_all = lax.all_gather(jnp.concatenate([r_share] * 4), "col")

    halves = call(
        pack_columns,
        (grid_cols, 2, 8, WIDE),
        [VMEM, VMEM],
        hamiltonian[:, :WIDE],
        factor_rows[:, :WIDE],
    )
    halves, r_share = lax.optimization_barrier((halves, r_share))
    halves = exchange(halves, "col")
    share = call(pack_share, (grid_rows, 4, 8, WIDE), [VMEM], halves[:2])
    shares = exchange(share, "row")
    offer = call(pack_gather, (grid_cols, 6, 8, WIDE), [SMEM, VMEM], place, shares)
    got = exchange(offer, "col")
    got, r_all = lax.optimization_barrier((got, r_all))
    cost = pl.CostEstimate(flops=10**9, bytes_accessed=5 * 10**6, transcendentals=0)
    return call(
        body,
        hamiltonian.shape,
        [SMEM, VMEM, VMEM, VMEM, pl.BlockSpec(memory_space=pl.ANY)],
        place,
        hamiltonian,
        factor_rows,
        got,
        r_all,
        cost_estimate=cost,
        scratch_shapes=[pltpu.VMEM((grid_cols, 8, hamiltonian.shape[1]), jnp.float32), pltpu.SemaphoreType.DMA],
    )


def solution(mesh):
    placed = (P("row", "col"), P(None, "col"))
    return jax.shard_map(
        per_device, mesh=mesh, in_specs=placed, out_specs=P("row", "col"), check_vma=False
    )
```

```python
import jax
import jax.numpy as jnp
from jax import lax
from jax.experimental import pallas as pl
from jax.experimental.pallas import tpu as pltpu
from jax.sharding import PartitionSpec as P

BLOCK = 64
WIDE = 2 * BLOCK
EXACT = lax.Precision.HIGHEST


def dot(left, right):
    return jnp.dot(left, right, precision=EXACT, preferred_element_type=jnp.float32)


def inner(left, right):
    return lax.dot_general(
        left, right, (((0,), (0,)), ((), ())), precision=EXACT, preferred_element_type=jnp.float32
    )


def halves_of(matrix):
    high = matrix.astype(jnp.bfloat16)
    return high, (matrix - high.astype(jnp.float32)).astype(jnp.bfloat16)


def split_dot(left, right):
    (left_high, left_low), (right_high, right_low) = left, right
    small = jnp.dot(left_high, right_low, preferred_element_type=jnp.float32)
    small += jnp.dot(left_low, right_high, preferred_element_type=jnp.float32)
    return small + jnp.dot(left_high, right_high, preferred_element_type=jnp.float32)


def wide_inverse(factor):
    row = lax.broadcasted_iota(jnp.int32, (WIDE, WIDE), 0)
    col = lax.broadcasted_iota(jnp.int32, (WIDE, WIDE), 1)
    on_diag = jnp.where(row == col, factor, 0.0)
    diag_col = jnp.sum(on_diag, axis=1, keepdims=True)
    diag_row = jnp.sum(on_diag, axis=0, keepdims=True)
    same = (row < BLOCK) == (col < BLOCK)
    power = jnp.where((row < col) & same, -factor / diag_col, 0.0)
    total = jnp.where(row == col, 1.0, power)
    power = dot(power, power)
    for _ in range(4):
        both = dot(jnp.concatenate([power, total], axis=0), power)
        power, total = both[:WIDE], total + both[WIDE:]
    total = (total + dot(total, power)) / diag_row
    couple = jnp.where((row < BLOCK) & (col >= BLOCK), factor, 0.0)
    return total - dot(total, dot(couple, total))


def beside(left, right):
    return jnp.concatenate([left, right], axis=1)


def owner_of(block):
    k = block // 4
    return (block + k) % 4, k


def pack_columns(h_hbm, r_hbm, out_ref, h_ref, r_ref, sems):
    first_lanes = pl.ds(0, WIDE)
    copies = [
        pltpu.make_async_copy(h_hbm.at[:, first_lanes], h_ref, sems.at[0]),
        pltpu.make_async_copy(r_hbm.at[:, first_lanes], r_ref, sems.at[1]),
    ]
    for copy in copies:
        copy.start()
    for copy in copies:
        copy.wait()
    h_cols, r_cols = h_ref[:, :BLOCK], r_ref[:, :BLOCK]
    first = h_cols[: 4 * BLOCK]
    second = jnp.concatenate([h_cols[7 * BLOCK : 8 * BLOCK], h_cols[4 * BLOCK : 7 * BLOCK]])
    third = jnp.concatenate([h_cols[10 * BLOCK :], h_cols[8 * BLOCK : 10 * BLOCK]])
    corner = jnp.concatenate([h_cols[:BLOCK], h_cols[:BLOCK], r_cols])
    out_ref[:, 0] = beside(first, second).reshape(-1, 8, WIDE)
    out_ref[:, 1] = beside(third, corner).reshape(-1, 8, WIDE)


def pack_share(halves_ref, out_ref):
    for slot in range(2):
        left, right = halves_ref[0, slot], halves_ref[1, slot]
        low = beside(left[:, :BLOCK], right[:, :BLOCK])
        high = beside(left[:, BLOCK:], right[:, BLOCK:])
        for row in range(out_ref.shape[0]):
            out_ref[row, 2 * slot] = low
            out_ref[row, 2 * slot + 1] = high


def pack_gather(place, all_ref, r_ref, out_ref):
    grid_row, grid_col = place[0], place[1]
    grid_rows, grid_cols = all_ref.shape[0], out_ref.shape[0]
    own = all_ref[grid_row]
    corner_from = jnp.minimum(grid_col // 8, 1)
    corner = all_ref[corner_from, 3]
    parity = lax.rem(grid_col // 8, 2)
    for col in range(grid_cols):
        section = col // grid_rows
        lead = jnp.where(parity == section, 0, 1)
        for k in range(3):
            out_ref[col, k] = own[k]
        out_ref[col, 3] = all_ref[col % grid_rows, lead]
        out_ref[col, 4] = all_ref[col % grid_rows, 2]
        out_ref[col, 5] = corner
        for k in range(3):
            out_ref[col, 6 + k] = r_ref[:, k * WIDE : (k + 1) * WIDE]


def body(place, h_ref, rj_ref, got_ref, out_hbm, out_ref, sems):
    grid_row, grid_col = place[0], place[1]
    width = rj_ref.shape[1]
    blocks = width // BLOCK
    corner = got_ref[:, 5].reshape(2, WIDE, WIDE)
    inverse = wide_inverse(corner[1])
    result = dot(inner(inverse, corner[0]), inverse)
    own_section = grid_col // 16
    h_own = []
    for m in range(blocks):
        (even, k), (odd, _) = owner_of(2 * m), owner_of(2 * m + 1)
        group = jnp.where(own_section == 0, even, odd)
        slot = 4 if k == 2 else 3
        h_own.append(got_ref[pl.ds(8 * group, 8), slot].reshape(BLOCK, WIDE))
    h_own = jnp.concatenate(h_own).T
    r_own = rj_ref[...]
    weights = beside(inverse.T, -0.5 * result)
    z_own = dot(weights, jnp.concatenate([h_own, r_own], axis=0))
    right = halves_of(jnp.concatenate([z_own, r_own], axis=0))
    across = jnp.concatenate([-0.5 * result.T, inverse], axis=0)
    lane = lax.broadcasted_iota(jnp.int32, (BLOCK, width), 1)
    inside = (lane >= BLOCK) | (grid_col >= 2)
    copies = []
    for section in (1, 0):
        r_piece = jnp.concatenate(
            [
                got_ref[16 * section : 16 * section + 16, 6 + k].reshape(WIDE, WIDE).T
                for k in range(width // WIDE)
            ]
        )
        h_piece = []
        for m in range(blocks):
            group, k = owner_of(2 * m + section)
            h_piece.append(got_ref[8 * group : 8 * group + 8, k].reshape(BLOCK, WIDE))
        z_piece = dot(beside(r_piece, jnp.concatenate(h_piece)), across)
        change = split_dot(halves_of(beside(r_piece, z_piece)), right)
        for m in range(blocks):
            rows = slice((2 * m + section) * BLOCK, (2 * m + section + 1) * BLOCK)
            part = change[m * BLOCK : (m + 1) * BLOCK]
            out_ref[rows, :] = h_ref[rows, :] - jnp.where(inside, part, 0.0)

        if section == 0:

            @pl.when(grid_row < 2)
            def _():
                pending = z_own - 0.5 * dot(result, r_own)
                old = h_ref[:BLOCK, :]
                first = grid_row == 0
                rest = jnp.where(first, pending[:BLOCK], pending[BLOCK:])
                lead = jnp.where(first, result[:BLOCK], result[BLOCK:])
                spread = jnp.concatenate([lead] * (width // WIDE), axis=1)
                turned = beside(lead[:, BLOCK:], lead[:, :BLOCK])
                turned = jnp.concatenate([turned] * (width // WIDE), axis=1)
                at_zero = jnp.where(first, spread, old)
                head = jnp.where(grid_col == 0, at_zero, turned)
                out_ref[:BLOCK, :] = jnp.where(inside, rest, head)

        for m in range(blocks):
            rows = pl.ds((2 * m + section) * BLOCK, BLOCK)
            copy = pltpu.make_async_copy(out_ref.at[rows], out_hbm.at[rows], sems.at[2 * m + section])
            copy.start()
            copies.append(copy)
    for copy in copies:
        copy.wait()


VMEM = pl.BlockSpec(memory_space=pltpu.VMEM)
SMEM = pl.BlockSpec(memory_space=pltpu.SMEM)
ANY = pl.BlockSpec(memory_space=pl.ANY)


def call(function, shape, specs, *operands, vmem=40, out=VMEM, **more):
    return pl.pallas_call(
        function,
        out_shape=jax.ShapeDtypeStruct(shape, jnp.float32),
        in_specs=specs,
        out_specs=out,
        compiler_params=pltpu.CompilerParams(vmem_limit_bytes=vmem * 1024 * 1024),
        **more,
    )(*operands)


def exchange(payload, axis):
    return lax.all_to_all(payload, axis, 0, 0)


def per_device(hamiltonian, factor_rows):
    grid_rows, grid_cols = lax.axis_size("row"), lax.axis_size("col")
    row_index, col_index = lax.axis_index("row"), lax.axis_index("col")
    place = jnp.stack([row_index, col_index])

    slab = WIDE // grid_rows
    pairs = [
        (r * grid_cols + c, (c % grid_rows) * grid_cols + grid_rows * (c // grid_rows) + r)
        for r in range(grid_rows)
        for c in range(grid_cols)
    ]
    r_slab = lax.dynamic_slice_in_dim(factor_rows, row_index * slab, slab, 0)
    r_share = lax.ppermute(r_slab, ("row", "col"), pairs)

    halves = call(
        pack_columns,
        (grid_cols, 2, 8, WIDE),
        [ANY, ANY],
        hamiltonian,
        factor_rows,
        vmem=58,
        scratch_shapes=[
            pltpu.VMEM((hamiltonian.shape[0], WIDE), jnp.float32),
            pltpu.VMEM((WIDE, WIDE), jnp.float32),
            pltpu.SemaphoreType.DMA((2,)),
        ],
    )
    halves = exchange(halves, "col")
    halves, r_share = lax.optimization_barrier((halves, r_share))
    share = call(pack_share, (grid_rows, 4, 8, WIDE), [VMEM], halves[:2])
    shares = exchange(share, "row")
    offer = call(pack_gather, (grid_cols, 9, 8, WIDE), [SMEM, VMEM, VMEM], place, shares, r_share)
    got = exchange(offer, "col")
    cost = pl.CostEstimate(flops=10**9, bytes_accessed=5 * 10**6, transcendentals=0)
    return call(
        body,
        hamiltonian.shape,
        [SMEM, VMEM, VMEM, VMEM],
        place,
        hamiltonian,
        factor_rows,
        got,
        cost_estimate=cost,
        out=ANY,
        scratch_shapes=[
            pltpu.VMEM(hamiltonian.shape, jnp.float32),
            pltpu.SemaphoreType.DMA((hamiltonian.shape[0] // BLOCK,)),
        ],
    )


def solution(mesh):
    placed = (P("row", "col"), P(None, "col"))
    return jax.shard_map(
        per_device, mesh=mesh, in_specs=placed, out_specs=P("row", "col"), check_vma=False
    )
```

```python
import jax
import jax.numpy as jnp
from jax import lax
from jax.experimental import pallas as pl
from jax.experimental.pallas import tpu as pltpu
from jax.sharding import PartitionSpec as P

BLOCK = 64
WIDE = 2 * BLOCK
EXACT = lax.Precision.HIGHEST


def dot(left, right):
    return jnp.dot(left, right, precision=EXACT, preferred_element_type=jnp.float32)


def inner(left, right):
    return lax.dot_general(
        left, right, (((0,), (0,)), ((), ())), precision=EXACT, preferred_element_type=jnp.float32
    )


def halves_of(matrix):
    high = matrix.astype(jnp.bfloat16)
    return high, (matrix - high.astype(jnp.float32)).astype(jnp.bfloat16)


def split_dot(left, right):
    (left_high, left_low), (right_high, right_low) = left, right
    small = jnp.dot(left_high, right_low, preferred_element_type=jnp.float32)
    small += jnp.dot(left_low, right_high, preferred_element_type=jnp.float32)
    return small + jnp.dot(left_high, right_high, preferred_element_type=jnp.float32)


def wide_inverse(factor):
    row = lax.broadcasted_iota(jnp.int32, (WIDE, WIDE), 0)
    col = lax.broadcasted_iota(jnp.int32, (WIDE, WIDE), 1)
    on_diag = jnp.where(row == col, factor, 0.0)
    diag_col = jnp.sum(on_diag, axis=1, keepdims=True)
    diag_row = jnp.sum(on_diag, axis=0, keepdims=True)
    same = (row < BLOCK) == (col < BLOCK)
    power = jnp.where((row < col) & same, -factor / diag_col, 0.0)
    total = jnp.where(row == col, 1.0, power)
    power = dot(power, power)
    for _ in range(4):
        both = dot(jnp.concatenate([power, total], axis=0), power)
        power, total = both[:WIDE], total + both[WIDE:]
    total = (total + dot(total, power)) / diag_row
    couple = jnp.where((row < BLOCK) & (col >= BLOCK), factor, 0.0)
    return total - dot(total, dot(couple, total))


def beside(left, right):
    return jnp.concatenate([left, right], axis=1)


def owner_of(block):
    k = block // 4
    return (block + k) % 4, k


def pack_columns(h_hbm, r_hbm, out_ref, h_ref, r_ref, sems):
    first_lanes = pl.ds(0, WIDE)
    copies = [
        pltpu.make_async_copy(h_hbm.at[:, first_lanes], h_ref, sems.at[0]),
        pltpu.make_async_copy(r_hbm.at[:, first_lanes], r_ref, sems.at[1]),
    ]
    for copy in copies:
        copy.start()
    for copy in copies:
        copy.wait()
    h_cols, r_cols = h_ref[:, :BLOCK], r_ref[:, :BLOCK]
    first = h_cols[: 4 * BLOCK]
    second = jnp.concatenate([h_cols[7 * BLOCK : 8 * BLOCK], h_cols[4 * BLOCK : 7 * BLOCK]])
    third = jnp.concatenate([h_cols[10 * BLOCK :], h_cols[8 * BLOCK : 10 * BLOCK]])
    corner = jnp.concatenate([h_cols[:BLOCK], h_cols[:BLOCK], r_cols])
    out_ref[:, 0] = beside(first, second).reshape(-1, 8, WIDE)
    out_ref[:, 1] = beside(third, corner).reshape(-1, 8, WIDE)


def pack_share(halves_ref, out_ref):
    for slot in range(2):
        left, right = halves_ref[0, slot], halves_ref[1, slot]
        low = beside(left[:, :BLOCK], right[:, :BLOCK])
        high = beside(left[:, BLOCK:], right[:, BLOCK:])
        for row in range(out_ref.shape[0]):
            out_ref[row, 2 * slot] = low
            out_ref[row, 2 * slot + 1] = high


def pack_gather(place, all_ref, r_ref, out_ref):
    grid_row, grid_col = place[0], place[1]
    grid_rows, grid_cols = all_ref.shape[0], out_ref.shape[0]
    own = all_ref[grid_row]
    corner_from = jnp.minimum(grid_col // 8, 1)
    corner = all_ref[corner_from, 3]
    parity = lax.rem(grid_col // 8, 2)
    for col in range(grid_cols):
        section = col // grid_rows
        lead = jnp.where(parity == section, 0, 1)
        for k in range(3):
            out_ref[col, k] = own[k]
        out_ref[col, 3] = all_ref[col % grid_rows, lead]
        out_ref[col, 4] = all_ref[col % grid_rows, 2]
        out_ref[col, 5] = corner
        for k in range(3):
            out_ref[col, 6 + k] = r_ref[:, k * WIDE : (k + 1) * WIDE]


def body(place, h_ref, rj_ref, got_ref, out_hbm, out_ref, sems):
    grid_row, grid_col = place[0], place[1]
    width = rj_ref.shape[1]
    blocks = width // BLOCK
    corner = got_ref[:, 5].reshape(2, WIDE, WIDE)
    inverse = wide_inverse(corner[1])
    result = dot(inner(inverse, corner[0]), inverse)
    own_section = grid_col // 16
    h_own = []
    for m in range(blocks):
        (even, k), (odd, _) = owner_of(2 * m), owner_of(2 * m + 1)
        group = jnp.where(own_section == 0, even, odd)
        slot = 4 if k == 2 else 3
        h_own.append(got_ref[pl.ds(8 * group, 8), slot].reshape(BLOCK, WIDE))
    h_own = jnp.concatenate(h_own).T
    r_own = rj_ref[...]
    weights = beside(inverse.T, -0.5 * result)
    z_own = dot(weights, jnp.concatenate([h_own, r_own], axis=0))
    right = halves_of(jnp.concatenate([z_own, r_own], axis=0))
    across = jnp.concatenate([-0.5 * result.T, inverse], axis=0)
    lane = lax.broadcasted_iota(jnp.int32, (BLOCK, width), 1)
    inside = (lane >= BLOCK) | (grid_col >= 2)
    copies = []
    for section in (1, 0):
        r_piece = jnp.concatenate(
            [
                got_ref[16 * section : 16 * section + 16, 6 + k].reshape(WIDE, WIDE).T
                for k in range(width // WIDE)
            ]
        )
        h_piece = []
        for m in range(blocks):
            group, k = owner_of(2 * m + section)
            h_piece.append(got_ref[8 * group : 8 * group + 8, k].reshape(BLOCK, WIDE))
        z_piece = dot(beside(r_piece, jnp.concatenate(h_piece)), across)
        change = split_dot(halves_of(beside(r_piece, z_piece)), right)
        for m in range(blocks):
            rows = slice((2 * m + section) * BLOCK, (2 * m + section + 1) * BLOCK)
            part = change[m * BLOCK : (m + 1) * BLOCK]
            out_ref[rows, :] = h_ref[rows, :] - jnp.where(inside, part, 0.0)

        if section == 0:

            @pl.when(grid_row < 2)
            def _():
                pending = z_own - 0.5 * dot(result, r_own)
                old = h_ref[:BLOCK, :]
                first = grid_row == 0
                rest = jnp.where(first, pending[:BLOCK], pending[BLOCK:])
                lead = jnp.where(first, result[:BLOCK], result[BLOCK:])
                spread = jnp.concatenate([lead] * (width // WIDE), axis=1)
                turned = beside(lead[:, BLOCK:], lead[:, :BLOCK])
                turned = jnp.concatenate([turned] * (width // WIDE), axis=1)
                at_zero = jnp.where(first, spread, old)
                head = jnp.where(grid_col == 0, at_zero, turned)
                out_ref[:BLOCK, :] = jnp.where(inside, rest, head)

        for m in range(blocks):
            rows = pl.ds((2 * m + section) * BLOCK, BLOCK)
            copy = pltpu.make_async_copy(out_ref.at[rows], out_hbm.at[rows], sems.at[2 * m + section])
            copy.start()
            copies.append(copy)
    for copy in copies:
        copy.wait()


VMEM = pl.BlockSpec(memory_space=pltpu.VMEM)
SMEM = pl.BlockSpec(memory_space=pltpu.SMEM)
ANY = pl.BlockSpec(memory_space=pl.ANY)


def call(function, shape, specs, *operands, vmem=40, out=VMEM, **more):
    return pl.pallas_call(
        function,
        out_shape=jax.ShapeDtypeStruct(shape, jnp.float32),
        in_specs=specs,
        out_specs=out,
        compiler_params=pltpu.CompilerParams(vmem_limit_bytes=vmem * 1024 * 1024),
        **more,
    )(*operands)


def exchange(payload, axis):
    return lax.all_to_all(payload, axis, 0, 0)


def per_device(hamiltonian, factor_rows):
    grid_rows, grid_cols = lax.axis_size("row"), lax.axis_size("col")
    row_index, col_index = lax.axis_index("row"), lax.axis_index("col")
    place = jnp.stack([row_index, col_index])

    slab = WIDE // grid_rows
    pairs = [
        (r * grid_cols + c, (c % grid_rows) * grid_cols + grid_rows * (c // grid_rows) + r)
        for r in range(grid_rows)
        for c in range(grid_cols)
    ]
    r_slab = lax.dynamic_slice_in_dim(factor_rows, row_index * slab, slab, 0)
    r_share = lax.ppermute(r_slab, ("row", "col"), pairs)

    halves = call(
        pack_columns,
        (grid_cols, 2, 8, WIDE),
        [ANY, ANY],
        hamiltonian,
        factor_rows,
        vmem=58,
        scratch_shapes=[
            pltpu.VMEM((hamiltonian.shape[0], WIDE), jnp.float32),
            pltpu.VMEM((WIDE, WIDE), jnp.float32),
            pltpu.SemaphoreType.DMA((2,)),
        ],
    )
    halves = exchange(halves, "col")
    share = call(pack_share, (grid_rows, 4, 8, WIDE), [VMEM], halves[:2])
    shares = exchange(share, "row")
    offer = call(pack_gather, (grid_cols, 9, 8, WIDE), [SMEM, VMEM, VMEM], place, shares, r_share)
    got = exchange(offer, "col")
    cost = pl.CostEstimate(flops=10**9, bytes_accessed=5 * 10**6, transcendentals=0)
    return call(
        body,
        hamiltonian.shape,
        [SMEM, VMEM, VMEM, VMEM],
        place,
        hamiltonian,
        factor_rows,
        got,
        cost_estimate=cost,
        out=ANY,
        scratch_shapes=[
            pltpu.VMEM(hamiltonian.shape, jnp.float32),
            pltpu.SemaphoreType.DMA((hamiltonian.shape[0] // BLOCK,)),
        ],
    )


def solution(mesh):
    placed = (P("row", "col"), P(None, "col"))
    return jax.shard_map(
        per_device, mesh=mesh, in_specs=placed, out_specs=P("row", "col"), check_vma=False
    )
```
